512 devices in a mesh: rows: 64 (over x, y, core), probe: 8 (over z).
Axes of the slice: x: 4, y: 8, z: 8, core: 2. Of those that a mesh axis runs over, the one named last changes fastest.
Arguments:
- targets: float32 [3, 65536], P(None, 'rows'), may hold values from 0 to 1
- sources: bfloat16 [3, 8192], P(None, 'rows'), may hold values from 0 to 1
- probes: bfloat16 [256, 8192], P('probe', 'rows'), may hold values from -6 to 6
- cluster_sizes: int32 [512], P(('rows', 'probe')), may hold values from 64 to 128, as said below
- leaf_ranks: int32 [512], P(('rows', 'probe')), may hold values from 128 to 256, as said below
Outputs:
- leaf_basis: float32 [256, 2, 65536], P(None, None, ('rows', 'probe'))
- top_factor: float32 [512, 256, 256], P(('rows', 'probe'))
The draws below stay inside these ranges and needn't reach their ends.
Inputs may be any that keep to these rules, and one draw needn't show every extreme that they name: `cluster_sizes`: some leaf uses all 128 points in every draw. `leaf_ranks`: some leaf keeps all 256 rows in every draw.
All inputs are finite; a program needn't handle non-finite values.
Results may differ from the reference program's by a relative error of at most 0.0033.
Values may be sent and summed in bfloat16 or wider, within the bound.
A program may use at most 64 MiB of HBM per device.

```python
import jax
import jax.numpy as jnp
from jax import lax

LEAF = 128
NPROBE = 256
NCOL = 8192
LEAVES = 512
NROWS = 65536
N_ROWS = 64
N_PROBE = 8


def draw_cluster_sizes(key, part):
    values = jax.random.randint(key, (LEAVES,), LEAF // 2, LEAF + 1)
    position = jax.random.randint(jax.random.fold_in(key, 7), (), 0, LEAVES)
    lowest = jax.random.randint(jax.random.fold_in(key, 11), (), 0, LEAVES)
    values = values.at[lowest].set(LEAF // 2)
    return values.at[position].set(LEAF).astype(jnp.int32)


def draw_leaf_ranks(key, part):
    values = jax.random.randint(key, (LEAVES,), NPROBE // 2, NPROBE + 1)
    position = jax.random.randint(jax.random.fold_in(key, 13), (), 0, LEAVES)
    return values.at[position].set(NPROBE).astype(jnp.int32)


def level_of(key, shape, cuts, low, top_value):
    loudness = 1.0
    for axis_at, shards_of in cuts:
        steps = jax.random.uniform(jax.random.fold_in(jax.random.fold_in(key, 6), axis_at), (shards_of,), jnp.float32, low / len(cuts), top_value / len(cuts))
        loudness = loudness * jnp.repeat(jnp.exp(steps), shape[axis_at] // shards_of).reshape((-1,) + (1,) * (len(shape) - 1 - axis_at))
    return loudness


def scatter_about(rng, dims, deviation, most, pieces=(), kind=jnp.bfloat16):
    loudness = level_of(rng, dims, pieces, -0.22, 0.18) if pieces else 1.0
    array = jax.random.normal(rng, dims, jnp.float32) * deviation * loudness
    return jnp.minimum(jnp.maximum(array, -most), most).astype(kind)


def setup_inputs(seed: int = 0) -> dict:
    splits = jax.random.split(jax.random.key(seed), 6)
    return {
        "targets": jnp.clip(1.0 * jax.random.uniform(splits[0], (3, NROWS), jnp.float32) ** level_of(splits[0], (3, NROWS), ((1, 64),), -0.2, 0.2), 0.0, 1.0),
        "sources": jnp.clip(1.0 * jax.random.uniform(splits[1], (3, NCOL), jnp.float32) ** level_of(splits[1], (3, NCOL), ((1, 64),), -0.2, 0.2), 0.0, 1.0).astype(jnp.bfloat16),
        "probes": scatter_about(splits[2], (NPROBE, NCOL), 1.0, 6.0, ((0, 8), (1, 64))),
        "cluster_sizes": draw_cluster_sizes(jax.random.fold_in(splits[5], 71), 0),
        "leaf_ranks": draw_leaf_ranks(jax.random.fold_in(splits[5], 71), 0),
    }


wavenumber = 30.0
softening = 0.02

def kernel_pair(source_pts, target_pts, col_total):
    diff_x = source_pts[0][:, None] - target_pts[0][None, :]
    diff_y = source_pts[1][:, None] - target_pts[1][None, :]
    diff_z = source_pts[2][:, None] - target_pts[2][None, :]
    distance = jnp.sqrt(diff_x * diff_x + diff_y * diff_y + diff_z * diff_z + softening * softening)
    amplitude = 1.0 / (distance * jnp.sqrt(jnp.float32(col_total)))
    kernel_cos = (amplitude * jnp.cos(wavenumber * distance)).astype(jnp.bfloat16)
    kernel_sin = (amplitude * jnp.sin(wavenumber * distance)).astype(jnp.bfloat16)
    return (kernel_cos, kernel_sin)

def cholesky_basis(matrix):
    gram_matrix = jnp.dot(matrix, matrix.T, precision=lax.Precision.HIGHEST)
    shift_value = jnp.trace(gram_matrix) / NPROBE
    factor = jnp.linalg.cholesky(gram_matrix + shift_value * jnp.eye(NPROBE, dtype=matrix.dtype))
    return jax.scipy.linalg.solve_triangular(factor, matrix, lower=True)

def merge_node(stacked):
    basis_rows = cholesky_basis(stacked)
    return jnp.dot(stacked, basis_rows.T, precision=lax.Precision.HIGHEST)

def merge_level(projected):
    left_part = projected[0::2]
    right_part = projected[1::2]
    stacked = jnp.concatenate([left_part, right_part], axis=-1)
    shape_kept = stacked.shape
    flat = stacked.reshape(-1, NPROBE, 2 * NPROBE)
    merged = lax.map(merge_node, flat)
    return merged.reshape(shape_kept[0], shape_kept[1], NPROBE, NPROBE)

def reference(targets, sources, probes, cluster_sizes, leaf_ranks):
    source_pts = sources.astype(jnp.float32)
    probe_vals = probes.astype(jnp.float32)

    def one_leaf(leaf_index):
        target_pts = lax.dynamic_slice_in_dim(targets, leaf_index * LEAF, LEAF, 1)
        kernel_cos, kernel_sin = kernel_pair(source_pts, target_pts, NCOL)
        sample_cos = jnp.dot(probe_vals, kernel_cos.astype(jnp.float32), precision=lax.Precision.HIGHEST)
        sample_sin = jnp.dot(probe_vals, kernel_sin.astype(jnp.float32), precision=lax.Precision.HIGHEST)
        kept_rows = (jnp.arange(LEAF) < cluster_sizes[leaf_index]).astype(jnp.float32)
        matrix = jnp.concatenate([sample_cos * kept_rows, sample_sin * kept_rows], axis=1)
        basis_rows = cholesky_basis(matrix)
        rank_rows = (jnp.arange(NPROBE) < leaf_ranks[leaf_index]).astype(jnp.float32)
        basis_rows = basis_rows * rank_rows[:, None]
        projected = jnp.dot(matrix, basis_rows.T, precision=lax.Precision.HIGHEST)
        return (basis_rows, projected)
    leaf_bases, leaf_projs = lax.map(one_leaf, jnp.arange(LEAVES, dtype=jnp.int32))
    leaf_basis = leaf_bases.reshape(LEAVES, NPROBE, 2, LEAF).transpose(1, 2, 0, 3).reshape(NPROBE, 2, NROWS)
    grouped = leaf_projs.reshape(N_ROWS, N_PROBE, NPROBE, NPROBE)
    level_one = merge_level(grouped)
    level_two = merge_level(level_one)
    top_factor = jnp.repeat(level_two, 4, axis=0).reshape(LEAVES, NPROBE, NPROBE)
    return (leaf_basis, top_factor)
```

```python
import functools
import math

import jax
import jax.numpy as jnp
from jax import lax
from jax.experimental import pallas as pl
from jax.experimental.pallas import tpu as pltpu
from jax.sharding import PartitionSpec as P

MESH = pl.DeviceIdType.MESH
BF = jnp.bfloat16
F32 = jnp.float32
WAVENUMBER = 30.0
SOFTENING = 0.02
NX, NY, NZ, NC = 4, 8, 8, 2
GROUPS = (2, 1, 3, 0)
RING = (4, 3, 5, 2, 6, 1, 7)
HALF = 16
LEAF = 128
NPROBE = 256
SPREAD = NPROBE + 2.0
SIN_TERMS = (3.1415926401839527, -5.167710090327096, 2.5500776596356878, -0.5982921588728, 0.07765940703413433)
COS_TERMS = (0.999999953466513, -4.934792858655427, 4.058411913769729, -1.3318801587034552, 0.2196967935096479)
NN = (((1,), (0,)), ((), ()))
NT = (((1,), (1,)), ((), ()))
TN = (((0,), (0,)), ((), ()))


def horner(terms, value, factor):
    total = terms[-1] * factor
    for term in terms[-2::-1]:
        total = total * value + term * factor
    return total


def sample_kernel(
    col_total, targets_ref, sources_ref, probes_ref, out_ref,
    tgt, src, spread, part_a, part_b, lhs, kmat, pair_out, own, pair_in, line_out, line_in,
    send_sem, recv_sem,
):
    r, z = lax.axis_index("rows"), lax.axis_index("probe")
    x, y, c = r // (NY * NC), (r // NC) % NY, r % NC

    def at(xx, yy, cc):
        return (xx * NY + yy) * NC + cc

    y_peer = {d: (at(x, lax.rem(y + d, NY), c), z) for d in range(1, NY)}
    z_peer = {d: (r, lax.rem(z + d, NZ)) for d in range(1, NZ)}
    xc_peer = {
        (dx, dc): (at(lax.rem(x + dx, NX), y, lax.rem(c + dc, NC)), z)
        for dx in range(NX) for dc in range(NC) if (dx, dc) != (0, 0)
    }
    peers = list(y_peer.values()) + list(z_peer.values()) + list(xc_peer.values())
    barrier = pltpu.get_barrier_semaphore()
    for peer in peers:
        pl.semaphore_signal(barrier, inc=1, device_id=peer, device_id_type=MESH)

    scale = WAVENUMBER / (2.0 * math.pi)
    pad = jnp.zeros((5, LEAF), F32)
    own_cols = pl.ds(pl.multiple_of(z * LEAF, LEAF), LEAF)
    tgt[x * NC + c] = jnp.concatenate([targets_ref[:, own_cols] * scale, pad], axis=0)
    src[y] = jnp.concatenate([sources_ref[...].astype(F32) * scale, pad], axis=0)
    part_a[y, z] = probes_ref[0:HALF, :]
    part_b[z, y] = probes_ref[HALF : 2 * HALF, :]
    pl.semaphore_wait(barrier, len(peers))

    slots = iter(range(64))

    def send(from_ref, to_ref, peer):
        slot = next(slots)
        copy = pltpu.make_async_remote_copy(
            src_ref=from_ref, dst_ref=to_ref, send_sem=send_sem.at[slot], recv_sem=recv_sem.at[slot],
            device_id=peer, device_id_type=MESH,
        )
        copy.start()
        return copy

    order = RING
    src_copies = [send(src.at[y], src.at[y], y_peer[d]) for d in order]
    tgt_copies = [send(tgt.at[x * NC + c], tgt.at[x * NC + c], peer) for peer in xc_peer.values()]
    a_copies = [send(part_a.at[y, z], part_a.at[y, z], z_peer[d]) for d in order]
    b_copies = [send(part_b.at[z, y], part_b.at[z, y], y_peer[d]) for d in order]

    for copy in src_copies:
        copy.wait_recv()
    for yy in range(NY):
        for axis in range(3):
            row = src[yy, axis : axis + 1, :]
            spread[axis, yy * LEAF : (yy + 1) * LEAF, :] = jnp.broadcast_to(row, (LEAF, LEAF)).T
    for copy in a_copies:
        copy.wait_recv()
    a2_copies = [send(part_a.at[y], part_a.at[y], y_peer[d]) for d in order]
    for copy in b_copies:
        copy.wait_recv()
    b2_copies = [send(part_b.at[z], part_b.at[z], z_peer[d]) for d in order]
    for copy in tgt_copies:
        copy.wait_recv()

    amp = scale / math.sqrt(col_total)
    root = math.sqrt(2.0 * amp)
    soft = (SOFTENING * scale) ** 2
    chunk = 64

    def fill(group):
        xx = lax.rem(x + GROUPS[group], NX)
        leaf = [tgt[xx * NC + lax.rem(c + 1, NC)], tgt[xx * NC + c]]

        def body(i, carry):
            rows = pl.ds(pl.multiple_of(i * chunk, chunk), chunk)
            for role in range(2):
                dx = spread[0, rows, :] - leaf[role][0:1, :]
                dy = spread[1, rows, :] - leaf[role][1:2, :]
                dz = spread[2, rows, :] - leaf[role][2:3, :]
                squared = (dx * dx + dy * dy) + (dz * dz + soft)
                inverse = lax.rsqrt(squared)
                turns = squared * inverse
                turns = turns - jnp.round(turns)
                t2 = turns * turns
                sine = turns * horner(SIN_TERMS, t2, root)
                cosine = horner(COS_TERMS, t2, root)
                lead = inverse * sine
                base = role * 2 * LEAF
                kmat[group, rows, base : base + LEAF] = (amp * inverse - lead * sine).astype(BF)
                kmat[group, rows, base + LEAF : base + 2 * LEAF] = (lead * cosine).astype(BF)
            return carry

        lax.fori_loop(0, NY * LEAF // chunk, body, 0)

    def multiply(group):
        part = jnp.dot(lhs[...], kmat[group], preferred_element_type=F32)
        pair_out[group] = part[:, : 2 * LEAF]
        own[group] = part[:, 2 * LEAF :]
        return send(pair_out.at[group], pair_in.at[group], xc_peer[(0, 1)])

    for group in range(len(GROUPS)):
        fill(group)
    for copy in a2_copies + b2_copies:
        copy.wait_recv()
    for yy in range(NY):
        cols = slice(yy * LEAF, (yy + 1) * LEAF)
        lhs[: NPROBE // 2, cols] = part_a[yy].reshape(NPROBE // 2, LEAF)
        lhs[NPROBE // 2 :, cols] = part_b[:, yy].reshape(NPROBE // 2, LEAF)
    pair_copies, line_copies = [], []

    def pass_on(group):
        pair_copies[group].wait_recv()
        line_out[group] = (own[group] + pair_in[group]).astype(line_out.dtype)
        line_copies.append(send(line_out.at[group], line_in.at[group], xc_peer[(GROUPS[group], 0)]))

    for group in range(len(GROUPS)):
        pair_copies.append(multiply(group))
        if group >= 1:
            pass_on(group - 1)
    pair_copies[3].wait_recv()
    total = own[3] + pair_in[3]
    for group in range(3):
        line_copies[group].wait_recv()
        total = total + line_in[group].astype(F32)
    for half in range(2):
        for zz in range(NZ):
            to, frm = (2 * zz + half) * HALF, (half * NZ + zz) * HALF
            out_ref[to : to + HALF, :] = total[frm : frm + HALF, :]
    for copy in src_copies + tgt_copies + a_copies + b_copies + a2_copies + b2_copies + pair_copies + line_copies:
        copy.wait_send()


def split(a):
    high = a.astype(BF)
    return high, (a - high.astype(F32)).astype(BF)


def mm(a, b, dims):
    return lax.dot_general(a, b, dims, preferred_element_type=F32)


def dot_split(a, b, dims=NN):
    (ah, al), (bh, bl) = a, b
    return mm(ah, bh, dims) + (mm(ah, bl, dims) + mm(al, bh, dims))


def dot3(a, b, dims=NN):
    return dot_split(split(a), split(b), dims)


def diagonal(n):
    return lax.broadcasted_iota(jnp.int32, (n, n), 0) == lax.broadcasted_iota(jnp.int32, (n, n), 1)


def eye(n):
    return diagonal(n).astype(F32)


def spd_inverses(mats, low):
    alpha = 2.0 / (1.0 + SPREAD)
    delta = (SPREAD - 1.0) / (SPREAD + 1.0)
    inv_low = 1.0 / low
    ids = [eye(m.shape[0]) for m in mats]
    rest = [i - (alpha * inv_low) * m for i, m in zip(ids, mats)]
    found = None
    while True:
        c = 2.0 / (2.0 - delta * delta)
        delta = delta * delta / (2.0 - delta * delta)
        parts = [split(v) for v in rest]
        if found is None:
            found = [(c * alpha) * (i + v) for i, v in zip(ids, rest)]
        else:
            found = [c * (f + dot_split(split(f), p)) for f, p in zip(found, parts)]
        if delta < 1e-5:
            return [f * inv_low for f in found]
        rest = [(1.0 - c) * i + c * dot_split(p, p) for i, p in zip(ids, parts)]


def lanes(tile, k):
    return jnp.broadcast_to(tile[:, k : k + 1], tile.shape)


def base_inverse(blocks, in_ref, out_ref, panel=8):
    n = blocks[0].shape[0]
    for b, block in enumerate(blocks):
        in_ref[:, b, :] = jnp.concatenate([block, eye(n)], axis=1)
    v = [in_ref[k] for k in range(n)]
    for k in range(0, n, panel):
        p = [[lanes(v[k + i], k + j) for j in range(i + 1)] for i in range(panel)]
        low = [[None] * panel for _ in range(panel)]
        r, x, u = [None] * panel, [None] * panel, [None] * panel
        for j in range(panel):
            r[j] = lax.rsqrt(p[j][j])
            x[j] = v[k + j] * r[j]
            out_ref[k + j] = x[j]
            for i in range(j + 1, panel):
                low[i][j] = p[i][j] * r[j]
            for i in range(j + 1, panel):
                for m in range(j + 1, i + 1):
                    p[i][m] = p[i][m] - low[i][j] * low[m][j]
                v[k + i] = v[k + i] - low[i][j] * x[j]
        for j in reversed(range(panel)):
            u[j] = x[j] * r[j]
            for m in range(j):
                x[m] = x[m] - low[j][m] * u[j]
        for i in range(k + panel, n):
            t = [lanes(v[i], k + j) * u[j] for j in range(panel)]
            while len(t) > 1:
                t = [a + b for a, b in zip(t[::2], t[1::2])]
            v[i] = v[i] - t[0]


BASE = 32
LINE = F32


def chol_inverse(h, low, in_ref, out_ref):
    level, stack = [h], []
    while level[0].shape[0] > BASE:
        m = level[0].shape[0] // 2
        a11 = [b[:m, :m] for b in level]
        a21 = [b[m:, :m] for b in level]
        inverses = spd_inverses(a11, low)
        w = [dot3(p, q) for p, q in zip(a21, inverses)]
        schur = [b[m:, m:] - dot3(q, p, NT) for b, q, p in zip(level, w, a21)]
        stack.append(w)
        level = [b for pair in zip(a11, schur) for b in pair]
    base_inverse(level, in_ref, out_ref)
    xs = [out_ref[:, i, :][:, BASE:] for i in range(len(level))]
    while stack:
        joined = []
        for i, w in enumerate(stack.pop()):
            first, second = xs[2 * i], xs[2 * i + 1]
            top = jnp.concatenate([first, jnp.zeros_like(first)], axis=1)
            joined.append(jnp.concatenate([top, jnp.concatenate([-dot3(second, w), second], axis=1)], axis=0))
        xs = joined
    return xs[0]


def shift_of(gram):
    kept = jnp.where(diagonal(NPROBE), gram, 0.0)
    return jnp.sum(jnp.sum(kept, axis=0, keepdims=True), axis=1, keepdims=True) * (1.0 / NPROBE)


def leaf_kernel(size_ref, rank_ref, samples_ref, basis_ref, gram_ref, in_ref, out_ref):
    col = lax.broadcasted_iota(jnp.int32, (NPROBE, 2 * LEAF), 1) % LEAF
    matrix = split(jnp.where(col < size_ref[0], samples_ref[...], 0.0))
    gram = dot_split(matrix, matrix, NT)
    shift = shift_of(gram)
    inverse = chol_inverse(gram + shift * eye(NPROBE), shift, in_ref, out_ref)
    row = lax.broadcasted_iota(jnp.int32, (NPROBE, NPROBE), 0)
    inverse = split(jnp.where(row < rank_ref[0], inverse, 0.0))
    projected = split(dot_split(inverse, split(gram)))
    gram_ref[...] = dot_split(projected, projected, TN)
    basis = dot_split(inverse, matrix)
    basis_ref[:, 0, :] = basis[:, :LEAF]
    basis_ref[:, 1, :] = basis[:, LEAF:]


def middle_kernel(left_ref, right_ref, gram_ref):
    gram = left_ref[...] + right_ref[...]
    shift = shift_of(gram)
    inverse = spd_inverses([gram + shift * eye(NPROBE)], shift)[0]
    gram_ref[...] = gram - shift * eye(NPROBE) + (shift * shift) * inverse


def top_kernel(left_ref, right_ref, top_ref, in_ref, out_ref):
    gram = left_ref[...] + right_ref[...]
    shift = shift_of(gram)
    inverse = chol_inverse(gram + shift * eye(NPROBE), shift, in_ref, out_ref)
    top_ref[0] = dot3(gram, inverse, NT)


def per_device(targets, sources, probes, cluster_sizes, leaf_ranks):
    col_total = sources.shape[1] * lax.axis_size("rows")
    square = jax.ShapeDtypeStruct((NPROBE, NPROBE), F32)
    vmem = pl.BlockSpec(memory_space=pltpu.VMEM)
    smem = pl.BlockSpec(memory_space=pltpu.SMEM)
    base = [pltpu.VMEM((BASE, 8, 2 * BASE), F32)] * 2
    samples = pl.pallas_call(
        functools.partial(sample_kernel, col_total),
        out_shape=square,
        in_specs=[vmem] * 3,
        out_specs=vmem,
        scratch_shapes=[
            pltpu.VMEM((NX * NC, 8, LEAF), F32),
            pltpu.VMEM((NY, 8, LEAF), F32),
            pltpu.VMEM((3, NY * LEAF, LEAF), F32),
            pltpu.VMEM((NY, NZ, HALF, LEAF), BF),
            pltpu.VMEM((NZ, NY, HALF, LEAF), BF),
            pltpu.VMEM((NPROBE, NY * LEAF), BF),
            pltpu.VMEM((4, NY * LEAF, 4 * LEAF), BF),
            pltpu.VMEM((4, NPROBE, 2 * LEAF), F32),
            pltpu.VMEM((4, NPROBE, 2 * LEAF), F32),
            pltpu.VMEM((4, NPROBE, 2 * LEAF), F32),
            pltpu.VMEM((3, NPROBE, 2 * LEAF), LINE),
            pltpu.VMEM((3, NPROBE, 2 * LEAF), LINE),
            pltpu.SemaphoreType.DMA((49,)),
            pltpu.SemaphoreType.DMA((49,)),
        ],
        compiler_params=pltpu.CompilerParams(
            collective_id=0, has_side_effects=True, vmem_limit_bytes=40 * 1024 * 1024
        ),
    )(targets, sources, probes)
    small = pltpu.CompilerParams(vmem_limit_bytes=40 * 1024 * 1024)
    basis, gram = pl.pallas_call(
        leaf_kernel,
        out_shape=(jax.ShapeDtypeStruct((NPROBE, 2, LEAF), F32), square),
        in_specs=[smem, smem, vmem],
        out_specs=(vmem, vmem),
        scratch_shapes=base,
        compiler_params=small,
    )(cluster_sizes, leaf_ranks, samples)
    pairs = [[(s, s ^ bit) for s in range(lax.axis_size("rows"))] for bit in (1, 2)]
    gram = pl.pallas_call(
        middle_kernel, out_shape=square, in_specs=[vmem] * 2, out_specs=vmem, compiler_params=small
    )(gram, lax.ppermute(gram, "rows", pairs[0]))
    top = pl.pallas_call(
        top_kernel,
        out_shape=jax.ShapeDtypeStruct((1, NPROBE, NPROBE), F32),
        in_specs=[vmem] * 2,
        out_specs=vmem,
        scratch_shapes=base,
        compiler_params=small,
    )(gram, lax.ppermute(gram, "rows", pairs[1]))
    return basis, top


def solution(mesh):
    return jax.shard_map(
        per_device,
        mesh=mesh,
        in_specs=(
            P(None, "rows"),
            P(None, "rows"),
            P("probe", "rows"),
            P(("rows", "probe")),
            P(("rows", "probe")),
        ),
        out_specs=(P(None, None, ("rows", "probe")), P(("rows", "probe"), None, None)),
        check_vma=False,
    )
```

```python
import functools
import math

import jax
import jax.numpy as jnp
from jax import lax
from jax.experimental import pallas as pl
from jax.experimental.pallas import tpu as pltpu
from jax.sharding import PartitionSpec as P

MESH = pl.DeviceIdType.MESH
BF = jnp.bfloat16
F32 = jnp.float32
WAVENUMBER = 30.0
SOFTENING = 0.02
NX, NY, NZ, NC = 4, 8, 8, 2
GROUPS = (2, 1, 3, 0)
RING = (4, 3, 5, 2, 6, 1, 7)
HALF = 16
LEAF = 128
NPROBE = 256
SPREAD = NPROBE + 2.0
SIN_TERMS = (3.1415926401839527, -5.167710090327096, 2.5500776596356878, -0.5982921588728, 0.07765940703413433)
COS_TERMS = (0.999999953466513, -4.934792858655427, 4.058411913769729, -1.3318801587034552, 0.2196967935096479)
NN = (((1,), (0,)), ((), ()))
NT = (((1,), (1,)), ((), ()))
TN = (((0,), (0,)), ((), ()))


def horner(terms, value, factor):
    total = terms[-1] * factor
    for term in terms[-2::-1]:
        total = total * value + term * factor
    return total


def sample_kernel(
    col_total, targets_ref, sources_ref, probes_ref, out_ref,
    tgt, src, spread, part_a, part_b, lhs, kmat, pair_out, own, pair_in, line_out, relay_in, line_in,
    send_sem, recv_sem,
):
    r, z = lax.axis_index("rows"), lax.axis_index("probe")
    x, y, c = r // (NY * NC), (r // NC) % NY, r % NC

    def at(xx, yy, cc):
        return (xx * NY + yy) * NC + cc

    y_peer = {d: (at(x, lax.rem(y + d, NY), c), z) for d in range(1, NY)}
    z_peer = {d: (r, lax.rem(z + d, NZ)) for d in range(1, NZ)}
    xc_peer = {
        (dx, dc): (at(lax.rem(x + dx, NX), y, lax.rem(c + dc, NC)), z)
        for dx in range(NX) for dc in range(NC) if (dx, dc) != (0, 0)
    }
    peers = list(y_peer.values()) + list(z_peer.values()) + list(xc_peer.values())
    barrier = pltpu.get_barrier_semaphore()
    for peer in peers:
        pl.semaphore_signal(barrier, inc=1, device_id=peer, device_id_type=MESH)

    scale = WAVENUMBER / (2.0 * math.pi)
    pad = jnp.zeros((5, LEAF), F32)
    own_cols = pl.ds(pl.multiple_of(z * LEAF, LEAF), LEAF)
    tgt[x * NC + c] = jnp.concatenate([targets_ref[:, own_cols] * scale, pad], axis=0)
    src[y] = jnp.concatenate([sources_ref[...].astype(F32) * scale, pad], axis=0)
    part_a[y, z] = probes_ref[0:HALF, :]
    part_b[z, y] = probes_ref[HALF : 2 * HALF, :]
    pl.semaphore_wait(barrier, len(peers))

    slots = iter(range(64))

    def send(from_ref, to_ref, peer):
        slot = next(slots)
        copy = pltpu.make_async_remote_copy(
            src_ref=from_ref, dst_ref=to_ref, send_sem=send_sem.at[slot], recv_sem=recv_sem.at[slot],
            device_id=peer, device_id_type=MESH,
        )
        copy.start()
        return copy

    order = RING
    src_copies = [send(src.at[y], src.at[y], y_peer[d]) for d in order]
    tgt_copies = [send(tgt.at[x * NC + c], tgt.at[x * NC + c], peer) for peer in xc_peer.values()]
    a_copies = [send(part_a.at[y, z], part_a.at[y, z], z_peer[d]) for d in order]
    b_copies = [send(part_b.at[z, y], part_b.at[z, y], y_peer[d]) for d in order]

    for copy in src_copies:
        copy.wait_recv()
    for yy in range(NY):
        for axis in range(3):
            row = src[yy, axis : axis + 1, :]
            spread[axis, yy * LEAF : (yy + 1) * LEAF, :] = jnp.broadcast_to(row, (LEAF, LEAF)).T
    for copy in a_copies:
        copy.wait_recv()
    a2_copies = [send(part_a.at[y], part_a.at[y], y_peer[d]) for d in order]
    for copy in b_copies:
        copy.wait_recv()
    b2_copies = [send(part_b.at[z], part_b.at[z], z_peer[d]) for d in order]
    for copy in tgt_copies:
        copy.wait_recv()

    amp = scale / math.sqrt(col_total)
    root = math.sqrt(2.0 * amp)
    soft = (SOFTENING * scale) ** 2
    chunk = 64

    def fill(group):
        xx = lax.rem(x + GROUPS[group], NX)
        leaf = [tgt[xx * NC + lax.rem(c + 1, NC)], tgt[xx * NC + c]]

        def body(i, carry):
            rows = pl.ds(pl.multiple_of(i * chunk, chunk), chunk)
            for role in range(2):
                dx = spread[0, rows, :] - leaf[role][0:1, :]
                dy = spread[1, rows, :] - leaf[role][1:2, :]
                dz = spread[2, rows, :] - leaf[role][2:3, :]
                squared = (dx * dx + dy * dy) + (dz * dz + soft)
                inverse = lax.rsqrt(squared)
                turns = squared * inverse
                turns = turns - jnp.round(turns)
                t2 = turns * turns
                sine = turns * horner(SIN_TERMS, t2, root)
                cosine = horner(COS_TERMS, t2, root)
                lead = inverse * sine
                base = role * 2 * LEAF
                kmat[group, rows, base : base + LEAF] = (amp * inverse - lead * sine).astype(BF)
                kmat[group, rows, base + LEAF : base + 2 * LEAF] = (lead * cosine).astype(BF)
            return carry

        lax.fori_loop(0, NY * LEAF // chunk, body, 0)

    def multiply(group):
        part = jnp.dot(lhs[...], kmat[group], preferred_element_type=F32)
        pair_out[group] = part[:, : 2 * LEAF]
        own[group] = part[:, 2 * LEAF :]
        return send(pair_out.at[group], pair_in.at[group], xc_peer[(0, 1)])

    for group in range(len(GROUPS)):
        fill(group)
    for copy in a2_copies + b2_copies:
        copy.wait_recv()
    for yy in range(NY):
        cols = slice(yy * LEAF, (yy + 1) * LEAF)
        lhs[: NPROBE // 2, cols] = part_a[yy].reshape(NPROBE // 2, LEAF)
        lhs[NPROBE // 2 :, cols] = part_b[:, yy].reshape(NPROBE // 2, LEAF)
    pair_copies, line_copies = [], []
    first, second = slice(0, NPROBE // 2), slice(NPROBE // 2, NPROBE)

    def sums(group, rows):
        return own[group, rows] + pair_in[group, rows]

    def line(slot, rows, value, to_ref, dx):
        line_out[slot, rows] = value
        copy = send(line_out.at[slot, rows], to_ref.at[rows], xc_peer[(dx, 0)])
        line_copies.append(copy)
        return copy

    for group in range(len(GROUPS)):
        pair_copies.append(multiply(group))
    pair_copies[0].wait_recv()
    relay = [line(0, first, sums(0, first), relay_in, 1), line(0, second, sums(0, second), relay_in, 3)]
    pair_copies[1].wait_recv()
    direct = [line(1, second, sums(1, second), line_in.at[0], 1)]
    pair_copies[2].wait_recv()
    direct.append(line(2, first, sums(2, first), line_in.at[1], 3))
    relay[0].wait_recv()
    direct.append(line(1, first, sums(1, first) + relay_in[first], line_in.at[0], 1))
    relay[1].wait_recv()
    direct.append(line(2, second, sums(2, second) + relay_in[second], line_in.at[1], 3))
    pair_copies[3].wait_recv()
    for copy in direct:
        copy.wait_recv()
    total = (own[3] + pair_in[3]) + (line_in[0] + line_in[1])
    for half in range(2):
        for zz in range(NZ):
            to, frm = (2 * zz + half) * HALF, (half * NZ + zz) * HALF
            out_ref[to : to + HALF, :] = total[frm : frm + HALF, :]
    for copy in src_copies + tgt_copies + a_copies + b_copies + a2_copies + b2_copies + pair_copies + line_copies:
        copy.wait_send()


def split(a):
    high = a.astype(BF)
    return high, (a - high.astype(F32)).astype(BF)


def mm(a, b, dims):
    return lax.dot_general(a, b, dims, preferred_element_type=F32)


def dot_split(a, b, dims=NN):
    (ah, al), (bh, bl) = a, b
    return mm(ah, bh, dims) + (mm(ah, bl, dims) + mm(al, bh, dims))


def dot3(a, b, dims=NN):
    return dot_split(split(a), split(b), dims)


def diagonal(n):
    return lax.broadcasted_iota(jnp.int32, (n, n), 0) == lax.broadcasted_iota(jnp.int32, (n, n), 1)


def eye(n):
    return diagonal(n).astype(F32)


def spd_inverses(mats, low):
    alpha = 2.0 / (1.0 + SPREAD)
    delta = (SPREAD - 1.0) / (SPREAD + 1.0)
    inv_low = 1.0 / low
    ids = [eye(m.shape[0]) for m in mats]
    rest = [i - (alpha * inv_low) * m for i, m in zip(ids, mats)]
    found = None
    while True:
        c = 2.0 / (2.0 - delta * delta)
        delta = delta * delta / (2.0 - delta * delta)
        parts = [split(v) for v in rest]
        if found is None:
            found = [(c * alpha) * (i + v) for i, v in zip(ids, rest)]
        else:
            found = [c * (f + dot_split(split(f), p)) for f, p in zip(found, parts)]
        if delta < 1e-5:
            return [f * inv_low for f in found]
        rest = [(1.0 - c) * i + c * dot_split(p, p) for i, p in zip(ids, parts)]


def lanes(tile, k):
    return jnp.broadcast_to(tile[:, k : k + 1], tile.shape)


def base_inverse(blocks, in_ref, out_ref, panel=8):
    n = blocks[0].shape[0]
    for b, block in enumerate(blocks):
        in_ref[:, b, :] = jnp.concatenate([block, eye(n)], axis=1)
    v = [in_ref[k] for k in range(n)]
    for k in range(0, n, panel):
        p = [[lanes(v[k + i], k + j) for j in range(i + 1)] for i in range(panel)]
        low = [[None] * panel for _ in range(panel)]
        r, x, u = [None] * panel, [None] * panel, [None] * panel
        for j in range(panel):
            r[j] = lax.rsqrt(p[j][j])
            x[j] = v[k + j] * r[j]
            out_ref[k + j] = x[j]
            for i in range(j + 1, panel):
                low[i][j] = p[i][j] * r[j]
            for i in range(j + 1, panel):
                for m in range(j + 1, i + 1):
                    p[i][m] = p[i][m] - low[i][j] * low[m][j]
                v[k + i] = v[k + i] - low[i][j] * x[j]
        for j in reversed(range(panel)):
            u[j] = x[j] * r[j]
            for m in range(j):
                x[m] = x[m] - low[j][m] * u[j]
        for i in range(k + panel, n):
            t = [lanes(v[i], k + j) * u[j] for j in range(panel)]
            while len(t) > 1:
                t = [a + b for a, b in zip(t[::2], t[1::2])]
            v[i] = v[i] - t[0]


BASE = 32


def chol_inverse(h, low, in_ref, out_ref):
    level, stack = [h], []
    while level[0].shape[0] > BASE:
        m = level[0].shape[0] // 2
        a11 = [b[:m, :m] for b in level]
        a21 = [b[m:, :m] for b in level]
        inverses = spd_inverses(a11, low)
        w = [dot3(p, q) for p, q in zip(a21, inverses)]
        schur = [b[m:, m:] - dot3(q, p, NT) for b, q, p in zip(level, w, a21)]
        stack.append(w)
        level = [b for pair in zip(a11, schur) for b in pair]
    base_inverse(level, in_ref, out_ref)
    xs = [out_ref[:, i, :][:, BASE:] for i in range(len(level))]
    while stack:
        joined = []
        for i, w in enumerate(stack.pop()):
            first, second = xs[2 * i], xs[2 * i + 1]
            top = jnp.concatenate([first, jnp.zeros_like(first)], axis=1)
            joined.append(jnp.concatenate([top, jnp.concatenate([-dot3(second, w), second], axis=1)], axis=0))
        xs = joined
    return xs[0]


def shift_of(gram):
    kept = jnp.where(diagonal(NPROBE), gram, 0.0)
    return jnp.sum(jnp.sum(kept, axis=0, keepdims=True), axis=1, keepdims=True) * (1.0 / NPROBE)


def tree_kernel(
    size_ref, rank_ref, samples_ref, basis_ref, top_ref,
    in_ref, out_ref, gram_out, gram_in, node_out, node_in, send_sem, recv_sem,
):
    r, z = lax.axis_index("rows"), lax.axis_index("probe")
    c, y = r % NC, (r // NC) % NY
    sibling = (r + 1 - 2 * c, z)
    cousin = (r + NC * (1 - 2 * (y % 2)), z)
    barrier = pltpu.get_barrier_semaphore()
    for peer in (sibling, cousin):
        pl.semaphore_signal(barrier, inc=1, device_id=peer, device_id_type=MESH)

    col = lax.broadcasted_iota(jnp.int32, (NPROBE, 2 * LEAF), 1) % LEAF
    matrix = split(jnp.where(col < size_ref[0], samples_ref[...], 0.0))
    gram = dot_split(matrix, matrix, NT)
    shift = shift_of(gram)
    inverse = chol_inverse(gram + shift * eye(NPROBE), shift, in_ref, out_ref)
    row = lax.broadcasted_iota(jnp.int32, (NPROBE, NPROBE), 0)
    inverse = split(jnp.where(row < rank_ref[0], inverse, 0.0))
    projected = split(dot_split(inverse, split(gram)))
    gram = dot_split(projected, projected, TN)
    gram_out[...] = gram
    pl.semaphore_wait(barrier, 2)

    def send(from_ref, to_ref, slot, peer):
        copy = pltpu.make_async_remote_copy(
            src_ref=from_ref, dst_ref=to_ref, send_sem=send_sem.at[slot], recv_sem=recv_sem.at[slot],
            device_id=peer, device_id_type=MESH,
        )
        copy.start()
        return copy

    pair = send(gram_out, gram_in, 0, sibling)
    basis = dot_split(inverse, matrix)
    basis_ref[:, 0, :] = basis[:, :LEAF]
    basis_ref[:, 1, :] = basis[:, LEAF:]
    pair.wait_recv()

    gram = gram + gram_in[...]
    shift = shift_of(gram)
    inverse = spd_inverses([gram + shift * eye(NPROBE)], shift)[0]
    gram = gram - shift * eye(NPROBE) + (shift * shift) * inverse
    half = NPROBE // 2
    node_out[0] = gram[:half, :half]
    node_out[1] = gram[half:, :half]
    node_out[2] = gram[half:, half:]
    node = send(node_out, node_in, 1, cousin)
    node.wait_recv()
    part = [node_out[i] + node_in[i] for i in range(3)]
    gram = jnp.concatenate(
        [jnp.concatenate([part[0], part[1].T], axis=1), jnp.concatenate([part[1], part[2]], axis=1)], axis=0
    )
    shift = shift_of(gram)
    inverse = chol_inverse(gram + shift * eye(NPROBE), shift, in_ref, out_ref)
    top_ref[0] = dot3(gram, inverse, NT)
    pair.wait_send()
    node.wait_send()


def per_device(targets, sources, probes, cluster_sizes, leaf_ranks):
    col_total = sources.shape[1] * lax.axis_size("rows")
    square = jax.ShapeDtypeStruct((NPROBE, NPROBE), F32)
    vmem = pl.BlockSpec(memory_space=pltpu.VMEM)
    smem = pl.BlockSpec(memory_space=pltpu.SMEM)
    base = [pltpu.VMEM((BASE, 8, 2 * BASE), F32)] * 2
    samples = pl.pallas_call(
        functools.partial(sample_kernel, col_total),
        out_shape=square,
        in_specs=[vmem] * 3,
        out_specs=vmem,
        scratch_shapes=[
            pltpu.VMEM((NX * NC, 8, LEAF), F32),
            pltpu.VMEM((NY, 8, LEAF), F32),
            pltpu.VMEM((3, NY * LEAF, LEAF), F32),
            pltpu.VMEM((NY, NZ, HALF, LEAF), BF),
            pltpu.VMEM((NZ, NY, HALF, LEAF), BF),
            pltpu.VMEM((NPROBE, NY * LEAF), BF),
            pltpu.VMEM((4, NY * LEAF, 4 * LEAF), BF),
            pltpu.VMEM((4, NPROBE, 2 * LEAF), F32),
            pltpu.VMEM((4, NPROBE, 2 * LEAF), F32),
            pltpu.VMEM((4, NPROBE, 2 * LEAF), F32),
            pltpu.VMEM((3, NPROBE, 2 * LEAF), F32),
            pltpu.VMEM((NPROBE, 2 * LEAF), F32),
            pltpu.VMEM((2, NPROBE, 2 * LEAF), F32),
            pltpu.SemaphoreType.DMA((52,)),
            pltpu.SemaphoreType.DMA((52,)),
        ],
        compiler_params=pltpu.CompilerParams(
            collective_id=0, has_side_effects=True, vmem_limit_bytes=40 * 1024 * 1024
        ),
    )(targets, sources, probes)
    half = NPROBE // 2
    return pl.pallas_call(
        tree_kernel,
        out_shape=(
            jax.ShapeDtypeStruct((NPROBE, 2, LEAF), F32), jax.ShapeDtypeStruct((1, NPROBE, NPROBE), F32),
        ),
        in_specs=[smem, smem, vmem],
        out_specs=(vmem, vmem),
        scratch_shapes=base + [
            pltpu.VMEM((NPROBE, NPROBE), F32),
            pltpu.VMEM((NPROBE, NPROBE), F32),
            pltpu.VMEM((3, half, half), F32),
            pltpu.VMEM((3, half, half), F32),
            pltpu.SemaphoreType.DMA((2,)),
            pltpu.SemaphoreType.DMA((2,)),
        ],
        compiler_params=pltpu.CompilerParams(
            collective_id=1, has_side_effects=True, vmem_limit_bytes=40 * 1024 * 1024
        ),
    )(cluster_sizes, leaf_ranks, samples)


def solution(mesh):
    return jax.shard_map(
        per_device,
        mesh=mesh,
        in_specs=(
            P(None, "rows"),
            P(None, "rows"),
            P("probe", "rows"),
            P(("rows", "probe")),
            P(("rows", "probe")),
        ),
        out_specs=(P(None, None, ("rows", "probe")), P(("rows", "probe"), None, None)),
        check_vma=False,
    )
```
